512 devices in a mesh: dp: 64 (over y, x, z_lo), seq: 8 (over z_hi, core).
Axes of the slice: x: 4, y: 8, z: 8 (z_hi: 4, z_lo: 2; z = z_hi * 2 + z_lo), core: 2. Of those that a mesh axis runs over, the one named last changes fastest.
Arguments:
- queries: bfloat16 [65536, 2048], P(('dp', 'seq')), may hold values from -12 to 12
- keys: bfloat16 [65536, 2048], P(('dp', 'seq')), may hold values from -6 to 6
- values: bfloat16 [65536, 2048], P(('dp', 'seq')), may hold values from -6 to 6
- d_queries: bfloat16 [65536, 2048], P(('dp', 'seq')), may hold values from -6 to 6
- d_keys: bfloat16 [65536, 2048], P(('dp', 'seq')), may hold values from -6 to 6
- d_values: bfloat16 [65536, 2048], P(('dp', 'seq')), may hold values from -6 to 6
- out_weight: bfloat16 [2048, 3072], P('dp', 'seq'), may hold values from -0.125 to 0.125
- tangent_coef: float32 [64], P('dp'), may hold values from 0.5 to 2
- loss_weight: float32 [64], P('dp'), may hold values from 0.1 to 3
Outputs:
- weight_grad: float32 [2048, 3072], P('dp', 'seq')
The draws below stay inside these ranges and needn't reach their ends.
All inputs are finite; a program needn't handle non-finite values.
Results may differ from the reference program's by a relative error of at most 0.014.
Values may be sent and summed in bfloat16 or wider, within the bound.
No kernel may reach another device: no remote copies, remote signals or barrier semaphores. Data moves between devices by JAX's collectives and lax.ppermute only.
A program may use at most 64 MiB of HBM per device.

```python
import math
import jax
import jax.numpy as jnp
from jax import lax

D = 3072
HEADS = 16
HEAD = 128
HD = 2048
S = 1024
CLIPS = 64
TOKENS = 65536


def paired_rows(key):
    base_q = jax.random.truncated_normal(jax.random.fold_in(key, 11), -6.0, 6.0, (TOKENS, HD), jnp.float32)
    base_k = jax.random.truncated_normal(jax.random.fold_in(key, 12), -6.0, 6.0, (TOKENS, HD), jnp.float32)
    key_rows = base_k
    query_rows = base_q
    return (query_rows, key_rows)


def draw_queries(key, part):
    query_rows, key_rows = paired_rows(key)
    return query_rows.astype(jnp.bfloat16)


def draw_keys(key, part):
    query_rows, key_rows = paired_rows(key)
    return key_rows.astype(jnp.bfloat16)


def steps_of(own_key, dims, shards, least, high):
    loudness, own = 1.0, jax.random.fold_in(own_key, 6)
    for position, blocks in shards:
        heights = jnp.exp(jax.random.uniform(jax.random.fold_in(own, position), (blocks,), jnp.float32, least / len(shards), high / len(shards)))
        loudness = loudness * jnp.repeat(heights, dims[position] // blocks).reshape([-1 if axis == position else 1 for axis in range(len(dims))])
    return loudness


def gaussian(stream_key, dims, width, most, pieces=(), held_as=jnp.bfloat16):
    result = jax.random.normal(stream_key, dims, jnp.float32) * width
    if len(pieces) > 0:
        result = steps_of(stream_key, dims, pieces, -0.22, 0.18) * result
    return jnp.clip(result, min=-most, max=most).astype(held_as)


def setup_inputs(seed: int = 0) -> dict:
    key_list = jax.random.split(jax.random.key(seed), 10)
    queries = draw_queries(jax.random.fold_in(key_list[9], 71), 0)
    keys = draw_keys(jax.random.fold_in(key_list[9], 71), 0)
    values = gaussian(key_list[2], (TOKENS, HD), 1.0, 6.0, ((0, 512),))
    d_queries = gaussian(key_list[3], (TOKENS, HD), 1.0, 6.0, ((0, 512),))
    d_keys = gaussian(key_list[4], (TOKENS, HD), 1.0, 6.0, ((0, 512),))
    d_values = gaussian(key_list[5], (TOKENS, HD), 1.0, 6.0, ((0, 512),))
    out_weight = gaussian(key_list[6], (HD, D), HD ** -0.5, 0.125, ((0, 64), (1, 8)))
    tangent_coef = jnp.clip(0.5 + 1.5 * jax.random.uniform(key_list[7], (CLIPS,), jnp.float32) ** steps_of(key_list[7], (CLIPS,), ((0, 64),), -0.2, 0.2), 0.5, 2.0)
    loss_weight = jnp.clip(jnp.exp(math.log(3.0) - 3.4011974 * jax.random.uniform(key_list[8], (CLIPS,), jnp.float32) ** steps_of(key_list[8], (CLIPS,), ((0, 64),), -0.2, 0.2)), 0.1, 3.0)
    return dict(queries=queries, keys=keys, values=values, d_queries=d_queries, d_keys=d_keys, d_values=d_values, out_weight=out_weight, tangent_coef=tangent_coef, loss_weight=loss_weight)


loss_scale = 64.0


def clip_terms(query, key, value, d_query, d_key, d_value, coef, weight, out_weight):
    shape = (S, HEADS, HEAD)
    q3 = query.reshape(shape).astype(jnp.float32)
    k3 = key.reshape(shape).astype(jnp.float32)
    v3 = value.reshape(shape).astype(jnp.float32)
    dq3 = d_query.reshape(shape).astype(jnp.float32)
    dk3 = d_key.reshape(shape).astype(jnp.float32)
    dv3 = d_value.reshape(shape).astype(jnp.float32)
    scale = 1.0 / (HEAD ** 0.5)
    scores = jnp.einsum("qhd,khd->hqk", q3, k3) * scale
    peak = jnp.max(scores, axis=-1, keepdims=True)
    expo = jnp.exp(scores - peak)
    probs = expo / jnp.sum(expo, axis=-1, keepdims=True)
    probs_low = probs.astype(jnp.bfloat16).astype(jnp.float32)
    attended = jnp.einsum("hqk,khd->qhd", probs_low, v3).astype(jnp.bfloat16)
    d_scores = (jnp.einsum("qhd,khd->hqk", dq3, k3) + jnp.einsum("qhd,khd->hqk", q3, dk3)) * scale
    d_probs = probs * (d_scores - jnp.sum(probs * d_scores, axis=-1, keepdims=True))
    d_low = d_probs.astype(jnp.bfloat16).astype(jnp.float32)
    d_attended = (jnp.einsum("hqk,khd->qhd", d_low, v3) + jnp.einsum("hqk,khd->qhd", probs_low, dv3)).astype(jnp.bfloat16)
    attended = attended.reshape(S, HD)
    d_attended = d_attended.reshape(S, HD)
    mixed = (attended.astype(jnp.float32) + coef * d_attended.astype(jnp.float32)).astype(jnp.bfloat16)
    projected = jnp.dot(mixed, out_weight, preferred_element_type=jnp.float32)
    residual_grad = (weight * projected).astype(jnp.bfloat16)
    return jnp.dot(attended.T, residual_grad, preferred_element_type=jnp.float32)


def reference(queries, keys, values, d_queries, d_keys, d_values, out_weight, tangent_coef, loss_weight):
    def split(x):
        return x.reshape(CLIPS, S, HD)

    def step(total, items):
        term = clip_terms(items[0], items[1], items[2], items[3], items[4], items[5], items[6], items[7], out_weight)
        return total + term, None

    start = jnp.zeros((HD, D), jnp.float32)
    total, _ = lax.scan(step, start, (split(queries), split(keys), split(values), split(d_queries), split(d_keys), split(d_values), tangent_coef, loss_weight))
    return total * (loss_scale / (TOKENS ** 0.5))
```

```python
import functools

import jax
import jax.numpy as jnp
from jax import lax
from jax.experimental import pallas as pl
from jax.experimental.pallas import tpu as pltpu
from jax.sharding import Mesh
from jax.sharding import PartitionSpec as P

HEAD = 128
LOSS_SCALE = 64.0
ROWS = 256
SEQ = ("zh", "core")
DP = ("y", "x", "zl")
NT = (((1,), (1,)), ((), ()))


def dot(a, b):
    return jnp.dot(a, b, preferred_element_type=jnp.float32)


def dot_nt(a, b):
    return lax.dot_general(a, b, NT, preferred_element_type=jnp.float32)


def flat(ref):
    return ref[...].reshape(-1, HEAD)


def probs_of(q, k, scale):
    scores = dot_nt(q, k) * scale
    expo = jnp.exp(scores - jnp.max(scores, axis=-1, keepdims=True))
    return expo / jnp.sum(expo, axis=-1, keepdims=True)


def forward_kernel(scale, q_ref, k_ref, v_ref, at_ref):
    low = probs_of(flat(q_ref), flat(k_ref), scale).astype(jnp.bfloat16)
    at_ref[...] = dot(low, flat(v_ref)).T.astype(jnp.bfloat16)


def tangent_kernel(
    scale, coef_ref, q_ref, k_ref, v_ref, dq_ref, dk_ref, dv_ref, mixed_ref
):
    q, k, v = flat(q_ref), flat(k_ref), flat(v_ref)
    probs = probs_of(q, k, scale)
    low = probs.astype(jnp.bfloat16)
    left = jnp.concatenate([flat(dq_ref), q], axis=1)
    right = jnp.concatenate([k, flat(dk_ref)], axis=1)
    d_scores = dot_nt(left, right) * scale
    shift = jnp.sum(probs * d_scores, axis=-1, keepdims=True)
    d_low = (probs * (d_scores - shift)).astype(jnp.bfloat16)
    tangent = (dot(d_low, v) + dot(low, flat(dv_ref))).astype(jnp.bfloat16)
    attended = dot(low, v).astype(jnp.bfloat16)
    mixed_ref[...] = (
        attended.astype(jnp.float32) + coef_ref[0] * tangent.astype(jnp.float32)
    ).astype(jnp.bfloat16)


def attention_specs(seq_count, tokens, arrays):
    per = ROWS // tokens
    query = lambda n: pl.BlockSpec((per, 1, tokens, HEAD), lambda h, i: (i, n, 0, h))
    whole = lambda n: pl.BlockSpec((seq_count, 1, tokens, HEAD), lambda h, i: (0, n, 0, h))
    return [query(0), whole(1), whole(2)] * arrays


def attend(qkv, scale):
    seq_count, _, tokens, width = qkv.shape
    length = seq_count * tokens
    return pl.pallas_call(
        functools.partial(forward_kernel, scale),
        grid=(width // HEAD, length // ROWS),
        in_specs=attention_specs(seq_count, tokens, 1),
        out_specs=pl.BlockSpec((HEAD, ROWS), lambda h, i: (h, i)),
        out_shape=jax.ShapeDtypeStruct((width, length), jnp.bfloat16),
        compiler_params=pltpu.CompilerParams(vmem_limit_bytes=32 << 20),
        cost_estimate=pl.CostEstimate(
            flops=8 * length * length * width, bytes_accessed=8 << 20, transcendentals=length * length * 2
        ),
        name="attend",
    )(qkv, qkv, qkv)


def attend_tangent(coef, qkv, d_qkv, scale):
    seq_count, _, tokens, width = qkv.shape
    length = seq_count * tokens
    return pl.pallas_call(
        functools.partial(tangent_kernel, scale),
        grid=(width // HEAD, length // ROWS),
        in_specs=[pl.BlockSpec(memory_space=pltpu.SMEM)] + attention_specs(seq_count, tokens, 2),
        out_specs=pl.BlockSpec((ROWS, HEAD), lambda h, i: (i, h)),
        out_shape=jax.ShapeDtypeStruct((length, width), jnp.bfloat16),
        compiler_params=pltpu.CompilerParams(vmem_limit_bytes=32 << 20),
        cost_estimate=pl.CostEstimate(
            flops=14 * length * length * width, bytes_accessed=8 << 20, transcendentals=length * length * 2
        ),
        name="tangent",
    )(coef, qkv, qkv, qkv, d_qkv, d_qkv, d_qkv)


def gram_kernel(count, weight_ref, place_ref, *refs):
    mixed_ref, out_ref = refs[-2], refs[-1]
    for n in range(count):
        out_ref[place_ref[n]] = weight_ref[0] * dot(refs[n][...], mixed_ref[...])


def gram(weight, place, blocks, mixed):
    count = len(blocks)
    rows, cols = blocks[0].shape[0], mixed.shape[1]
    smem = pl.BlockSpec(memory_space=pltpu.SMEM)
    vmem = pl.BlockSpec(memory_space=pltpu.VMEM)
    return pl.pallas_call(
        functools.partial(gram_kernel, count),
        in_specs=[smem, smem] + [vmem] * (count + 1),
        out_specs=vmem,
        out_shape=jax.ShapeDtypeStruct((count, rows, cols), jnp.float32),
        compiler_params=pltpu.CompilerParams(vmem_limit_bytes=32 << 20),
        name="gram",
    )(weight, place, *blocks, mixed)


def finish_kernel(factor, g_ref, w_ref, out_ref):
    total = jnp.zeros(out_ref.shape, jnp.float32)
    for n in range(g_ref.shape[0]):
        high = g_ref[n].astype(jnp.bfloat16)
        rest = (g_ref[n] - high.astype(jnp.float32)).astype(jnp.bfloat16)
        total = total + dot(high, w_ref[n]) + dot(rest, w_ref[n])
    out_ref[...] = total * factor


def finish(g, w, factor):
    return pl.pallas_call(
        functools.partial(finish_kernel, factor),
        out_shape=jax.ShapeDtypeStruct((g.shape[1], w.shape[2]), jnp.float32),
        compiler_params=pltpu.CompilerParams(vmem_limit_bytes=32 << 20),
        name="finish",
    )(g, w)


def shift(x, step):
    n = lax.axis_size("zh")
    return lax.ppermute(x, "zh", [(i, (i + step) % n) for i in range(n)])


def swap(x):
    return lax.ppermute(x, "core", [(0, 1), (1, 0)])


def gather_blocks(x):
    half = x.shape[0] // 2
    before, after = shift(x, 1), shift(x, -1)
    far = jnp.concatenate([shift(before[:half], 1), shift(after[half:], -1)], axis=0)
    own = [x, before, after, far]
    other = [swap(b) for b in own]
    zh, core = lax.axis_index("zh"), lax.axis_index("core")
    places = []
    for c in (core, 1 - core):
        for step in (0, 3, 1, 2):
            places.append(((zh + step) % 4) * 2 + c)
    return own + other, jnp.stack(places).astype(jnp.int32)


def to_heads(arrays, seq_count):
    stacked = jnp.stack(
        [x.reshape(x.shape[0], seq_count, -1).transpose(1, 0, 2) for x in arrays], axis=1
    )
    return lax.all_to_all(stacked, SEQ, split_axis=0, concat_axis=0, tiled=True)


def shards(
    queries, keys, values, d_queries, d_keys, d_values, out_weight, tangent_coef, loss_weight
):
    seq_count = lax.axis_size(SEQ)
    dp_count = lax.axis_size(DP)
    length = queries.shape[0] * seq_count
    scale = 1.0 / HEAD**0.5

    qkv = to_heads((queries, keys, values), seq_count)
    d_qkv = to_heads((d_queries, d_keys, d_values), seq_count)

    weight_all = lax.all_gather(out_weight, "zl", axis=0, tiled=True)
    weight_all = lax.all_gather(weight_all, "x", axis=0, tiled=True)
    weight_all = lax.all_gather(weight_all, "y", axis=0, tiled=True)

    attended_t = attend(qkv, scale)
    blocks, place = gather_blocks(attended_t)
    mixed = attend_tangent(tangent_coef, qkv, d_qkv, scale)
    term = gram(loss_weight, place, blocks, mixed)
    width = mixed.shape[1]
    parts = lax.all_to_all(
        term.reshape(dp_count, -1, width), DP, split_axis=0, concat_axis=0, tiled=True
    )
    summed = jnp.sum(parts, axis=0)
    rows = lax.all_to_all(
        jnp.broadcast_to(summed[None], (seq_count,) + summed.shape),
        SEQ,
        split_axis=0,
        concat_axis=0,
        tiled=True,
    )
    total_tokens = length * dp_count
    return finish(
        rows, weight_all.reshape(seq_count, width, -1), LOSS_SCALE / total_tokens**0.5
    )


def solution(mesh):
    split = Mesh(mesh.devices.reshape(8, 4, 2, 4, 2), DP + SEQ)
    tokens = P(DP + SEQ, None)
    placed = (tokens,) * 6 + (P(DP, SEQ), P(DP), P(DP))
    return jax.shard_map(
        shards, mesh=split, in_specs=placed, out_specs=P(DP, SEQ), check_vma=False
    )
```

```python
import functools

import jax
import jax.numpy as jnp
from jax import lax
from jax.experimental import pallas as pl
from jax.experimental.pallas import tpu as pltpu
from jax.sharding import Mesh
from jax.sharding import PartitionSpec as P

HEAD = 128
LOSS_SCALE = 64.0
ROWS = 256
HALVES = 2
STEPS = (0, 3, 1, 2)
SEQ = ("zh", "core")
NEAR = ("x", "zl")
DP = ("y", "x", "zl")
NT = (((1,), (1,)), ((), ()))


def dot(a, b):
    return jnp.dot(a, b, preferred_element_type=jnp.float32)


def dot_nt(a, b):
    return lax.dot_general(a, b, NT, preferred_element_type=jnp.float32)


def flat(ref):
    return ref[...].reshape(-1, HEAD)


def probs_of(q, k, scale):
    scores = dot_nt(q, k) * scale
    expo = jnp.exp(scores - jnp.max(scores, axis=-1, keepdims=True))
    return expo / jnp.sum(expo, axis=-1, keepdims=True)


def forward_kernel(scale, q_ref, k_ref, v_ref, at_ref):
    low = probs_of(flat(q_ref), flat(k_ref), scale).astype(jnp.bfloat16)
    at_ref[...] = dot(low, flat(v_ref)).T.astype(jnp.bfloat16)


def tangent_kernel(
    scale, coef_ref, q_ref, k_ref, v_ref, dq_ref, dk_ref, dv_ref, mixed_ref
):
    q, k, v = flat(q_ref), flat(k_ref), flat(v_ref)
    probs = probs_of(q, k, scale)
    low = probs.astype(jnp.bfloat16)
    left = jnp.concatenate([flat(dq_ref), q], axis=1)
    right = jnp.concatenate([k, flat(dk_ref)], axis=1)
    d_scores = dot_nt(left, right) * scale
    shift = jnp.sum(probs * d_scores, axis=-1, keepdims=True)
    d_low = (probs * (d_scores - shift)).astype(jnp.bfloat16)
    tangent = (dot(d_low, v) + dot(low, flat(dv_ref))).astype(jnp.bfloat16)
    attended = dot(low, v).astype(jnp.bfloat16)
    mixed_ref[...] = (
        attended.astype(jnp.float32) + coef_ref[0] * tangent.astype(jnp.float32)
    ).astype(jnp.bfloat16)


def attention_specs(seq_count, tokens, arrays, head=0):
    per = ROWS // tokens
    query = lambda n: pl.BlockSpec((per, 1, tokens, HEAD), lambda h, i: (i, n, 0, h + head))
    whole = lambda n: pl.BlockSpec(
        (seq_count, 1, tokens, HEAD), lambda h, i: (0, n, 0, h + head)
    )
    return [query(0), whole(1), whole(2)] * arrays


def attend(qkv, head, scale):
    seq_count, _, tokens, _ = qkv.shape
    length = seq_count * tokens
    return pl.pallas_call(
        functools.partial(forward_kernel, scale),
        grid=(1, length // ROWS),
        in_specs=attention_specs(seq_count, tokens, 1, head),
        out_specs=pl.BlockSpec((HEAD, ROWS), lambda h, i: (h, i)),
        out_shape=jax.ShapeDtypeStruct((HEAD, length), jnp.bfloat16),
        compiler_params=pltpu.CompilerParams(vmem_limit_bytes=8 << 20),
        cost_estimate=pl.CostEstimate(
            flops=4 * length * length * HEAD, bytes_accessed=2 << 20, transcendentals=length * length
        ),
        name="attend",
    )(qkv, qkv, qkv)


def attend_tangent(coef, qkv, d_qkv, scale):
    seq_count, _, tokens, width = qkv.shape
    length = seq_count * tokens
    return pl.pallas_call(
        functools.partial(tangent_kernel, scale),
        grid=(width // HEAD, length // ROWS),
        in_specs=[pl.BlockSpec(memory_space=pltpu.SMEM)] + attention_specs(seq_count, tokens, 2),
        out_specs=pl.BlockSpec((ROWS, HEAD), lambda h, i: (i, h)),
        out_shape=jax.ShapeDtypeStruct((length, width), jnp.bfloat16),
        compiler_params=pltpu.CompilerParams(vmem_limit_bytes=12 << 20),
        cost_estimate=pl.CostEstimate(
            flops=14 * length * length * width, bytes_accessed=8 << 20, transcendentals=length * length * 2
        ),
        name="tangent",
    )(coef, qkv, qkv, qkv, d_qkv, d_qkv, d_qkv)


def gram_kernel(weight_ref, at_ref, *refs):
    blocks, (own, other), out_ref = refs[: 4 * HALVES], refs[4 * HALVES : -2], refs[-1]
    near, depth, cols = out_ref.shape
    zh, core = at_ref[0], at_ref[1]
    part = blocks[0].shape[0] * HALVES // near
    span = near // HALVES
    peak = jnp.zeros((1, 1), jnp.float32)
    for n, step in enumerate(STEPS):
        chip = lax.rem(zh + step, 4)
        for half in range(HALVES):
            left = blocks[n * HALVES + half][...]
            for mixed_ref, side in ((own, core), (other, 1 - core)):
                block = weight_ref[0] * dot(left, mixed_ref[...])
                start = pl.multiple_of((chip * 2 + side) * part, part)
                out_ref[half * span : (half + 1) * span, pl.ds(start, part)] = block.reshape(
                    span, part, cols
                )
                peak = jnp.maximum(peak, jnp.max(jnp.abs(block), keepdims=True))
    out_ref[:, depth - 8 :] = jnp.broadcast_to(peak, (near, 8, cols))


def gram(weight, blocks, mixed, pieces, after):
    rows, cols = blocks[0].shape[0], mixed[0].shape[1]
    depth = 2 * len(blocks) * rows // pieces + 8
    at = jnp.stack([lax.axis_index("zh"), lax.axis_index("core")]).astype(jnp.int32)
    smem = pl.BlockSpec(memory_space=pltpu.SMEM)
    vmem = pl.BlockSpec(memory_space=pltpu.VMEM)
    return pl.pallas_call(
        gram_kernel,
        in_specs=[smem, smem] + [vmem] * (len(blocks) + 2) + [pl.BlockSpec(memory_space=pl.ANY)],
        out_specs=vmem,
        out_shape=jax.ShapeDtypeStruct((pieces, depth, cols), jnp.float32),
        compiler_params=pltpu.CompilerParams(vmem_limit_bytes=12 << 20),
        name="gram",
    )(weight, at, *blocks, *mixed, after)


def finish_kernel(factor, g_ref, w_ref, out_ref):
    total = jnp.zeros(out_ref.shape, jnp.float32)
    for n in range(g_ref.shape[0]):
        high = g_ref[n].astype(jnp.bfloat16)
        rest = (g_ref[n] - high.astype(jnp.float32)).astype(jnp.bfloat16)
        total = total + dot(high, w_ref[n]) + dot(rest, w_ref[n])
    out_ref[...] = total * factor


def finish(g, w, factor):
    return pl.pallas_call(
        functools.partial(finish_kernel, factor),
        out_shape=jax.ShapeDtypeStruct((g.shape[1], w.shape[2]), jnp.float32),
        compiler_params=pltpu.CompilerParams(vmem_limit_bytes=8 << 20),
        name="finish",
    )(g, w)


def shift(x, step):
    n = lax.axis_size("zh")
    return lax.ppermute(x, "zh", [(i, (i + step) % n) for i in range(n)])


def swap(x):
    return lax.ppermute(x, "core", [(0, 1), (1, 0)])


def neighbours(x):
    return shift(x, 1), shift(x, -1)


def settle(x):
    pairs = []
    for y in range(0, lax.axis_size("y"), 2):
        low, high = y * 2 + 1, (y + 1) * 2
        pairs += [(low, high), (high, low)]
    moved = lax.ppermute(x, ("y", "core"), pairs)
    stays = lax.axis_index("y") % 2 == lax.axis_index("core")
    return jnp.where(stays, x, moved)


def exchange(x, axes):
    return lax.all_to_all(x, axes, split_axis=0, concat_axis=0, tiled=True)


def by_heads(arrays, seq_count):
    return jnp.stack(
        [x.reshape(x.shape[0], seq_count, -1).transpose(1, 0, 2) for x in arrays], axis=1
    )


def reduce_near(term):
    count = term.shape[1] - 8
    power = jnp.ceil(jnp.log2(jnp.maximum(term[0, count, 0], 1e-30))) - 15.0
    row = lax.broadcasted_iota(jnp.int32, term.shape, 1)
    held = jnp.where(row < count, term * jnp.exp2(-power), power).astype(jnp.float16)
    parts = exchange(held, NEAR).astype(jnp.float32)
    return jnp.sum(parts[:, :count] * jnp.exp2(parts[:, count : count + 1, :1]), axis=0)


def shards(
    queries, keys, values, d_queries, d_keys, d_values, out_weight, tangent_coef, loss_weight
):
    seq_count = lax.axis_size(SEQ)
    dp_count = lax.axis_size(DP)
    length = queries.shape[0] * seq_count
    scale = 1.0 / HEAD**0.5

    qkv = by_heads((queries, keys, values), seq_count)
    d_qkv = by_heads((d_queries, d_keys, d_values), seq_count)
    pair = lax.all_gather(out_weight, "zl", axis=0, tiled=True)
    qkv, pair = lax.optimization_barrier((qkv, pair))
    weight_part = lax.all_gather(pair, "x", axis=0, tiled=True)
    d_qkv, weight_part = lax.optimization_barrier((d_qkv, weight_part))
    weight_all = lax.all_gather(weight_part, "y", axis=0, tiled=True)
    qkv, d_qkv = exchange(qkv, SEQ), exchange(d_qkv, SEQ)
    first, second = attend(qkv, 0, scale), attend(qkv, 1, scale)
    before_first, after_first = neighbours(first)
    before_second, after_second = neighbours(second)
    mixed = attend_tangent(tangent_coef, qkv, d_qkv, scale)
    before_first, before_second, after_first, after_second, mixed = lax.optimization_barrier(
        (before_first, before_second, after_first, after_second, mixed)
    )
    mixed_pair = (mixed, swap(mixed))
    far_first, far_second = shift(before_first, 1), shift(after_second, -1)
    blocks = (
        first, second, before_first, before_second,
        after_first, after_second, far_first, far_second,
    )
    term = gram(loss_weight, blocks, mixed_pair, lax.axis_size(NEAR), weight_all[:16, :HEAD])
    summed = reduce_near(term).reshape(lax.axis_size("y"), -1, mixed.shape[1])
    summed = settle(jnp.sum(exchange(summed, "y"), axis=0))
    rows = exchange(jnp.broadcast_to(summed[None], (seq_count,) + summed.shape), SEQ)
    total_tokens = length * dp_count
    return finish(
        rows, weight_all.reshape(seq_count, mixed.shape[1], -1), LOSS_SCALE / total_tokens**0.5
    )


def solution(mesh):
    split = Mesh(mesh.devices.reshape(8, 4, 2, 4, 2), DP + SEQ)
    tokens = P(DP + SEQ, None)
    placed = (tokens,) * 6 + (P(DP, SEQ), P(DP), P(DP))
    return jax.shard_map(
        shards, mesh=split, in_specs=placed, out_specs=P(DP, SEQ), check_vma=False
    )
```

```python
import functools

import jax
import jax.numpy as jnp
from jax import lax
from jax.experimental import pallas as pl
from jax.experimental.pallas import tpu as pltpu
from jax.sharding import Mesh
from jax.sharding import PartitionSpec as P

HEAD = 128
LOSS_SCALE = 64.0
ROWS = 256
HALVES = 2
STEPS = (0, 3, 1, 2)
SEQ = ("zh", "core")
NEAR = ("x", "zl")
DP = ("y", "x", "zl")
NT = (((1,), (1,)), ((), ()))


def dot(a, b):
    return jnp.dot(a, b, preferred_element_type=jnp.float32)


def dot_nt(a, b):
    return lax.dot_general(a, b, NT, preferred_element_type=jnp.float32)


def flat(ref):
    return ref[...].reshape(-1, HEAD)


def probs_of(q, k, scale):
    scores = dot_nt(q, k) * scale
    expo = jnp.exp(scores - jnp.max(scores, axis=-1, keepdims=True))
    return expo / jnp.sum(expo, axis=-1, keepdims=True)


def forward_kernel(scale, q_ref, k_ref, v_ref, at_ref):
    low = probs_of(flat(q_ref), flat(k_ref), scale).astype(jnp.bfloat16)
    at_ref[...] = dot(low, flat(v_ref)).T.astype(jnp.bfloat16)


def tangent_kernel(
    scale, coef_ref, q_ref, k_ref, v_ref, dq_ref, dk_ref, dv_ref, mixed_ref
):
    q, k, v = flat(q_ref), flat(k_ref), flat(v_ref)
    probs = probs_of(q, k, scale)
    low = probs.astype(jnp.bfloat16)
    left = jnp.concatenate([flat(dq_ref), q], axis=1)
    right = jnp.concatenate([k, flat(dk_ref)], axis=1)
    d_scores = dot_nt(left, right) * scale
    shift = jnp.sum(probs * d_scores, axis=-1, keepdims=True)
    d_low = (probs * (d_scores - shift)).astype(jnp.bfloat16)
    tangent = (dot(d_low, v) + dot(low, flat(dv_ref))).astype(jnp.bfloat16)
    attended = dot(low, v).astype(jnp.bfloat16)
    mixed_ref[...] = (
        attended.astype(jnp.float32) + coef_ref[0] * tangent.astype(jnp.float32)
    ).astype(jnp.bfloat16)


def attention_specs(seq_count, tokens, arrays, head=0):
    per = ROWS // tokens
    query = lambda n: pl.BlockSpec((per, 1, tokens, HEAD), lambda h, i: (i, n, 0, h + head))
    whole = lambda n: pl.BlockSpec(
        (seq_count, 1, tokens, HEAD), lambda h, i: (0, n, 0, h + head)
    )
    return [query(0), whole(1), whole(2)] * arrays


def attend(qkv, head, scale):
    seq_count, _, tokens, _ = qkv.shape
    length = seq_count * tokens
    return pl.pallas_call(
        functools.partial(forward_kernel, scale),
        grid=(1, length // ROWS),
        in_specs=attention_specs(seq_count, tokens, 1, head),
        out_specs=pl.BlockSpec((HEAD, ROWS), lambda h, i: (h, i)),
        out_shape=jax.ShapeDtypeStruct((HEAD, length), jnp.bfloat16),
        compiler_params=pltpu.CompilerParams(vmem_limit_bytes=8 << 20),
        cost_estimate=pl.CostEstimate(
            flops=4 * length * length * HEAD, bytes_accessed=2 << 20, transcendentals=length * length
        ),
        name="attend",
    )(qkv, qkv, qkv)


def attend_tangent(coef, qkv, d_qkv, scale):
    seq_count, _, tokens, width = qkv.shape
    length = seq_count * tokens
    return pl.pallas_call(
        functools.partial(tangent_kernel, scale),
        grid=(width // HEAD, length // ROWS),
        in_specs=[pl.BlockSpec(memory_space=pltpu.SMEM)] + attention_specs(seq_count, tokens, 2),
        out_specs=pl.BlockSpec((ROWS, HEAD), lambda h, i: (i, h)),
        out_shape=jax.ShapeDtypeStruct((length, width), jnp.bfloat16),
        compiler_params=pltpu.CompilerParams(vmem_limit_bytes=12 << 20),
        cost_estimate=pl.CostEstimate(
            flops=14 * length * length * width, bytes_accessed=8 << 20, transcendentals=length * length * 2
        ),
        name="tangent",
    )(coef, qkv, qkv, qkv, d_qkv, d_qkv, d_qkv)


def gram_kernel(weight_ref, at_ref, *refs):
    blocks, (own, other), out_ref = refs[: 4 * HALVES], refs[4 * HALVES : -2], refs[-1]
    near, depth, cols = out_ref.shape
    zh, core = at_ref[0], at_ref[1]
    part = blocks[0].shape[0] * HALVES // near
    span = near // HALVES
    peak = jnp.zeros((1, 1), jnp.float32)
    for n, step in enumerate(STEPS):
        chip = lax.rem(zh + step, 4)
        for half in range(HALVES):
            left = blocks[n * HALVES + half][...]
            for mixed_ref, side in ((own, core), (other, 1 - core)):
                block = weight_ref[0] * dot(left, mixed_ref[...])
                start = pl.multiple_of((chip * 2 + side) * part, part)
                out_ref[half * span : (half + 1) * span, pl.ds(start, part)] = block.reshape(
                    span, part, cols
                )
                peak = jnp.maximum(peak, jnp.max(jnp.abs(block), keepdims=True))
    out_ref[:, depth - 8 :] = jnp.broadcast_to(peak, (near, 8, cols))


def gram(weight, blocks, mixed, pieces, after):
    rows, cols = blocks[0].shape[0], mixed[0].shape[1]
    depth = 2 * len(blocks) * rows // pieces + 8
    at = jnp.stack([lax.axis_index("zh"), lax.axis_index("core")]).astype(jnp.int32)
    smem = pl.BlockSpec(memory_space=pltpu.SMEM)
    vmem = pl.BlockSpec(memory_space=pltpu.VMEM)
    return pl.pallas_call(
        gram_kernel,
        in_specs=[smem, smem] + [vmem] * (len(blocks) + 2) + [pl.BlockSpec(memory_space=pl.ANY)],
        out_specs=vmem,
        out_shape=jax.ShapeDtypeStruct((pieces, depth, cols), jnp.float32),
        compiler_params=pltpu.CompilerParams(vmem_limit_bytes=12 << 20),
        name="gram",
    )(weight, at, *blocks, *mixed, after)


def finish_kernel(factor, g_ref, w_ref, out_ref):
    total = jnp.zeros(out_ref.shape, jnp.float32)
    for n in range(g_ref.shape[0]):
        high = g_ref[n].astype(jnp.bfloat16)
        rest = (g_ref[n] - high.astype(jnp.float32)).astype(jnp.bfloat16)
        total = total + dot(high, w_ref[n]) + dot(rest, w_ref[n])
    out_ref[...] = total * factor


def finish(g, w, factor):
    return pl.pallas_call(
        functools.partial(finish_kernel, factor),
        out_shape=jax.ShapeDtypeStruct((g.shape[1], w.shape[2]), jnp.float32),
        compiler_params=pltpu.CompilerParams(vmem_limit_bytes=8 << 20),
        name="finish",
    )(g, w)


def shift(x, step):
    n = lax.axis_size("zh")
    return lax.ppermute(x, "zh", [(i, (i + step) % n) for i in range(n)])


def swap(x):
    return lax.ppermute(x, "core", [(0, 1), (1, 0)])


def neighbours(x):
    return shift(x, 1), shift(x, -1)


def settle(x):
    pairs = []
    for y in range(0, lax.axis_size("y"), 2):
        low, high = y * 2 + 1, (y + 1) * 2
        pairs += [(low, high), (high, low)]
    moved = lax.ppermute(x, ("y", "core"), pairs)
    stays = lax.axis_index("y") % 2 == lax.axis_index("core")
    return jnp.where(stays, x, moved)


def exchange(x, axes):
    return lax.all_to_all(x, axes, split_axis=0, concat_axis=0, tiled=True)


def by_heads(arrays, seq_count):
    return jnp.stack(
        [x.reshape(x.shape[0], seq_count, -1).transpose(1, 0, 2) for x in arrays], axis=1
    )


def reduce_near(term):
    count = term.shape[1] - 8
    power = jnp.ceil(jnp.log2(jnp.maximum(term[0, count, 0], 1e-30))) - 15.0
    row = lax.broadcasted_iota(jnp.int32, term.shape, 1)
    held = jnp.where(row < count, term * jnp.exp2(-power), power).astype(jnp.float16)
    parts = exchange(held, NEAR).astype(jnp.float32)
    return jnp.sum(parts[:, :count] * jnp.exp2(parts[:, count : count + 1, :1]), axis=0)


def shards(
    queries, keys, values, d_queries, d_keys, d_values, out_weight, tangent_coef, loss_weight
):
    seq_count = lax.axis_size(SEQ)
    dp_count = lax.axis_size(DP)
    length = queries.shape[0] * seq_count
    scale = 1.0 / HEAD**0.5

    qkv = by_heads((queries, keys, values), seq_count)
    d_qkv = by_heads((d_queries, d_keys, d_values), seq_count)
    weight_part = lax.all_gather(out_weight, "x", axis=0)
    d_qkv, weight_part = lax.optimization_barrier((d_qkv, weight_part))
    weight_part = lax.all_gather(weight_part, "zl", axis=1)
    weight_part = weight_part.reshape(-1, out_weight.shape[1])
    d_qkv, weight_part = lax.optimization_barrier((d_qkv, weight_part))
    weight_all = lax.all_gather(weight_part, "y", axis=0, tiled=True)
    qkv, d_qkv = exchange(qkv, SEQ), exchange(d_qkv, SEQ)
    first, second = attend(qkv, 0, scale), attend(qkv, 1, scale)
    before_first, after_first = neighbours(first)
    before_second, after_second = neighbours(second)
    mixed = attend_tangent(tangent_coef, qkv, d_qkv, scale)
    before_first, before_second, after_first, after_second, mixed = lax.optimization_barrier(
        (before_first, before_second, after_first, after_second, mixed)
    )
    mixed_pair = (mixed, swap(mixed))
    far_first, far_second = shift(before_first, 1), shift(after_second, -1)
    blocks = (
        first, second, before_first, before_second,
        after_first, after_second, far_first, far_second,
    )
    term = gram(loss_weight, blocks, mixed_pair, lax.axis_size(NEAR), weight_all[:16, :HEAD])
    summed = reduce_near(term).reshape(lax.axis_size("y"), -1, mixed.shape[1])
    summed = settle(jnp.sum(exchange(summed, "y"), axis=0))
    rows = exchange(jnp.broadcast_to(summed[None], (seq_count,) + summed.shape), SEQ)
    total_tokens = length * dp_count
    return finish(
        rows, weight_all.reshape(seq_count, mixed.shape[1], -1), LOSS_SCALE / total_tokens**0.5
    )


def solution(mesh):
    split = Mesh(mesh.devices.reshape(8, 4, 2, 4, 2), DP + SEQ)
    tokens = P(DP + SEQ, None)
    placed = (tokens,) * 6 + (P(DP, SEQ), P(DP), P(DP))
    return jax.shard_map(
        shards, mesh=split, in_specs=placed, out_specs=P(DP, SEQ), check_vma=False
    )
```

```python
import functools

import jax
import jax.numpy as jnp
from jax import lax
from jax.experimental import pallas as pl
from jax.experimental.pallas import tpu as pltpu
from jax.sharding import Mesh
from jax.sharding import PartitionSpec as P

HEAD = 128
LOSS_SCALE = 64.0
ROWS = 256
HALVES = 2
STEPS = (0, 3, 1, 2)
SEQ = ("zh", "core")
NEAR = ("x", "zl")
DP = ("y", "x", "zl")
NT = (((1,), (1,)), ((), ()))


def dot(a, b):
    return jnp.dot(a, b, preferred_element_type=jnp.float32)


def dot_nt(a, b):
    return lax.dot_general(a, b, NT, preferred_element_type=jnp.float32)


def flat(ref):
    return ref[...].reshape(-1, HEAD)


def probs_of(q, k, scale):
    scores = dot_nt(q, k) * scale
    expo = jnp.exp(scores - jnp.max(scores, axis=-1, keepdims=True))
    return expo / jnp.sum(expo, axis=-1, keepdims=True)


def forward_kernel(scale, q_ref, k_ref, v_ref, at_ref):
    low = probs_of(flat(q_ref), flat(k_ref), scale).astype(jnp.bfloat16)
    at_ref[...] = dot(low, flat(v_ref)).T.astype(jnp.bfloat16)


def tangent_kernel(
    scale, coef_ref, q_ref, k_ref, v_ref, dq_ref, dk_ref, dv_ref, mixed_ref
):
    q, k, v = flat(q_ref), flat(k_ref), flat(v_ref)
    probs = probs_of(q, k, scale)
    low = probs.astype(jnp.bfloat16)
    left = jnp.concatenate([flat(dq_ref), q], axis=1)
    right = jnp.concatenate([k, flat(dk_ref)], axis=1)
    d_scores = dot_nt(left, right) * scale
    shift = jnp.sum(probs * d_scores, axis=-1, keepdims=True)
    d_low = (probs * (d_scores - shift)).astype(jnp.bfloat16)
    tangent = (dot(d_low, v) + dot(low, flat(dv_ref))).astype(jnp.bfloat16)
    attended = dot(low, v).astype(jnp.bfloat16)
    mixed_ref[...] = (
        attended.astype(jnp.float32) + coef_ref[0] * tangent.astype(jnp.float32)
    ).astype(jnp.bfloat16)


def attention_specs(seq_count, tokens, arrays, head=0):
    per = ROWS // tokens
    query = lambda n: pl.BlockSpec((per, 1, tokens, HEAD), lambda h, i: (i, n, 0, h + head))
    whole = lambda n: pl.BlockSpec(
        (seq_count, 1, tokens, HEAD), lambda h, i: (0, n, 0, h + head)
    )
    return [query(0), whole(1), whole(2)] * arrays


def attend(qkv, head, scale):
    seq_count, _, tokens, _ = qkv.shape
    length = seq_count * tokens
    return pl.pallas_call(
        functools.partial(forward_kernel, scale),
        grid=(1, length // ROWS),
        in_specs=attention_specs(seq_count, tokens, 1, head),
        out_specs=pl.BlockSpec((HEAD, ROWS), lambda h, i: (h, i)),
        out_shape=jax.ShapeDtypeStruct((HEAD, length), jnp.bfloat16),
        compiler_params=pltpu.CompilerParams(vmem_limit_bytes=8 << 20),
        cost_estimate=pl.CostEstimate(
            flops=4 * length * length * HEAD, bytes_accessed=2 << 20, transcendentals=length * length
        ),
        name="attend",
    )(qkv, qkv, qkv)


def attend_tangent(coef, qkv, d_qkv, scale):
    seq_count, _, tokens, width = qkv.shape
    length = seq_count * tokens
    return pl.pallas_call(
        functools.partial(tangent_kernel, scale),
        grid=(width // HEAD, length // ROWS),
        in_specs=[pl.BlockSpec(memory_space=pltpu.SMEM)] + attention_specs(seq_count, tokens, 2),
        out_specs=pl.BlockSpec((ROWS, HEAD), lambda h, i: (i, h)),
        out_shape=jax.ShapeDtypeStruct((length, width), jnp.bfloat16),
        compiler_params=pltpu.CompilerParams(vmem_limit_bytes=12 << 20),
        cost_estimate=pl.CostEstimate(
            flops=14 * length * length * width, bytes_accessed=8 << 20, transcendentals=length * length * 2
        ),
        name="tangent",
    )(coef, qkv, qkv, qkv, d_qkv, d_qkv, d_qkv)


def gram_kernel(weight_ref, at_ref, *refs):
    blocks, (own, other), out_ref = refs[: 4 * HALVES], refs[4 * HALVES : -2], refs[-1]
    near, depth, cols = out_ref.shape
    zh, core = at_ref[0], at_ref[1]
    part = blocks[0].shape[0] * HALVES // near
    span = near // HALVES
    peak = jnp.zeros((1, 1), jnp.float32)
    for n, step in enumerate(STEPS):
        chip = lax.rem(zh + step, 4)
        for half in range(HALVES):
            left = blocks[n * HALVES + half][...]
            for mixed_ref, side in ((own, core), (other, 1 - core)):
                block = weight_ref[0] * dot(left, mixed_ref[...])
                start = pl.multiple_of((chip * 2 + side) * part, part)
                out_ref[half * span : (half + 1) * span, pl.ds(start, part)] = block.reshape(
                    span, part, cols
                )
                peak = jnp.maximum(peak, jnp.max(jnp.abs(block), keepdims=True))
    out_ref[:, depth - 8 :] = jnp.broadcast_to(peak, (near, 8, cols))


def gram(weight, blocks, mixed, pieces, after):
    rows, cols = blocks[0].shape[0], mixed[0].shape[1]
    depth = 2 * len(blocks) * rows // pieces + 8
    at = jnp.stack([lax.axis_index("zh"), lax.axis_index("core")]).astype(jnp.int32)
    smem = pl.BlockSpec(memory_space=pltpu.SMEM)
    vmem = pl.BlockSpec(memory_space=pltpu.VMEM)
    return pl.pallas_call(
        gram_kernel,
        in_specs=[smem, smem] + [vmem] * (len(blocks) + 2) + [pl.BlockSpec(memory_space=pl.ANY)],
        out_specs=vmem,
        out_shape=jax.ShapeDtypeStruct((pieces, depth, cols), jnp.float32),
        compiler_params=pltpu.CompilerParams(vmem_limit_bytes=12 << 20),
        name="gram",
    )(weight, at, *blocks, *mixed, after)


def finish_kernel(factor, g_ref, w_ref, out_ref):
    total = jnp.zeros(out_ref.shape, jnp.float32)
    for n in range(g_ref.shape[0]):
        high = g_ref[n].astype(jnp.bfloat16)
        rest = (g_ref[n] - high.astype(jnp.float32)).astype(jnp.bfloat16)
        total = total + dot(high, w_ref[n]) + dot(rest, w_ref[n])
    out_ref[...] = total * factor


def finish(g, w, factor):
    return pl.pallas_call(
        functools.partial(finish_kernel, factor),
        out_shape=jax.ShapeDtypeStruct((g.shape[1], w.shape[2]), jnp.float32),
        compiler_params=pltpu.CompilerParams(vmem_limit_bytes=8 << 20),
        name="finish",
    )(g, w)


def shift(x, step):
    n = lax.axis_size("zh")
    return lax.ppermute(x, "zh", [(i, (i + step) % n) for i in range(n)])


def swap(x):
    return lax.ppermute(x, "core", [(0, 1), (1, 0)])


def neighbours(x):
    return shift(x, 1), shift(x, -1)


def settle(x):
    pairs = []
    for y in range(0, lax.axis_size("y"), 2):
        low, high = y * 2 + 1, (y + 1) * 2
        pairs += [(low, high), (high, low)]
    moved = lax.ppermute(x, ("y", "core"), pairs)
    stays = lax.axis_index("y") % 2 == lax.axis_index("core")
    return jnp.where(stays, x, moved)


def gather_rows(x):
    mine = exchange(jnp.broadcast_to(x[None], (lax.axis_size("zh"),) + x.shape), "zh")
    theirs = swap(mine)
    first = lax.axis_index("core") == 0
    pair = (jnp.where(first, mine, theirs), jnp.where(first, theirs, mine))
    return jnp.stack(pair, axis=1).reshape((-1,) + x.shape)


def exchange(x, axes):
    return lax.all_to_all(x, axes, split_axis=0, concat_axis=0, tiled=True)


def by_heads(arrays, seq_count):
    return jnp.stack(
        [x.reshape(x.shape[0], seq_count, -1).transpose(1, 0, 2) for x in arrays], axis=1
    )


def reduce_near(term):
    count = term.shape[1] - 8
    power = jnp.ceil(jnp.log2(jnp.maximum(term[0, count, 0], 1e-30))) - 15.0
    row = lax.broadcasted_iota(jnp.int32, term.shape, 1)
    held = jnp.where(row < count, term * jnp.exp2(-power), power).astype(jnp.float16)
    parts = exchange(held, NEAR).astype(jnp.float32)
    return jnp.sum(parts[:, :count] * jnp.exp2(parts[:, count : count + 1, :1]), axis=0)


def shards(
    queries, keys, values, d_queries, d_keys, d_values, out_weight, tangent_coef, loss_weight
):
    seq_count = lax.axis_size(SEQ)
    dp_count = lax.axis_size(DP)
    length = queries.shape[0] * seq_count
    scale = 1.0 / HEAD**0.5

    qkv = by_heads((queries, keys, values), seq_count)
    d_qkv = by_heads((d_queries, d_keys, d_values), seq_count)
    weight_part = lax.all_gather(out_weight, "x", axis=0)
    d_qkv, weight_part = lax.optimization_barrier((d_qkv, weight_part))
    weight_part = lax.all_gather(weight_part, "zl", axis=1)
    weight_part = weight_part.reshape(-1, out_weight.shape[1])
    d_qkv, weight_part = lax.optimization_barrier((d_qkv, weight_part))
    weight_all = lax.all_gather(weight_part, "y", axis=0, tiled=True)
    qkv, d_qkv = exchange(qkv, SEQ), exchange(d_qkv, SEQ)
    first, second = attend(qkv, 0, scale), attend(qkv, 1, scale)
    before_first, after_first = neighbours(first)
    before_second, after_second = neighbours(second)
    mixed = attend_tangent(tangent_coef, qkv, d_qkv, scale)
    before_first, before_second, after_first, after_second, mixed = lax.optimization_barrier(
        (before_first, before_second, after_first, after_second, mixed)
    )
    mixed_pair = (mixed, swap(mixed))
    far_first, far_second = shift(before_first, 1), shift(after_second, -1)
    blocks = (
        first, second, before_first, before_second,
        after_first, after_second, far_first, far_second,
    )
    term = gram(loss_weight, blocks, mixed_pair, lax.axis_size(NEAR), weight_all[:16, :HEAD])
    summed = reduce_near(term).reshape(lax.axis_size("y"), -1, mixed.shape[1])
    summed = settle(jnp.sum(exchange(summed, "y"), axis=0))
    rows = gather_rows(summed)
    total_tokens = length * dp_count
    return finish(
        rows, weight_all.reshape(seq_count, mixed.shape[1], -1), LOSS_SCALE / total_tokens**0.5
    )


def solution(mesh):
    split = Mesh(mesh.devices.reshape(8, 4, 2, 4, 2), DP + SEQ)
    tokens = P(DP + SEQ, None)
    placed = (tokens,) * 6 + (P(DP, SEQ), P(DP), P(DP))
    return jax.shard_map(
        shards, mesh=split, in_specs=placed, out_specs=P(DP, SEQ), check_vma=False
    )
```

```python
import functools

import jax
import jax.numpy as jnp
from jax import lax
from jax.experimental import pallas as pl
from jax.experimental.pallas import tpu as pltpu
from jax.sharding import Mesh
from jax.sharding import PartitionSpec as P

HEAD = 128
LOSS_SCALE = 64.0
ROWS = 256
HALVES = 2
STEPS = (0, 3, 1, 2)
SEQ = ("zh", "core")
NEAR = ("x", "zl")
DP = ("y", "x", "zl")
NT = (((1,), (1,)), ((), ()))


def dot(a, b):
    return jnp.dot(a, b, preferred_element_type=jnp.float32)


def dot_nt(a, b):
    return lax.dot_general(a, b, NT, preferred_element_type=jnp.float32)


def flat(ref):
    return ref[...].reshape(-1, HEAD)


def probs_of(q, k, scale):
    scores = dot_nt(q, k) * scale
    expo = jnp.exp(scores - jnp.max(scores, axis=-1, keepdims=True))
    return expo / jnp.sum(expo, axis=-1, keepdims=True)


def forward_kernel(scale, q_ref, k_ref, v_ref, at_ref):
    low = probs_of(flat(q_ref), flat(k_ref), scale).astype(jnp.bfloat16)
    at_ref[...] = dot(low, flat(v_ref)).T.astype(jnp.bfloat16)


def tangent_kernel(
    scale, coef_ref, q_ref, k_ref, v_ref, dq_ref, dk_ref, dv_ref, mixed_ref
):
    q, k, v = flat(q_ref), flat(k_ref), flat(v_ref)
    probs = probs_of(q, k, scale)
    low = probs.astype(jnp.bfloat16)
    left = jnp.concatenate([flat(dq_ref), q], axis=1)
    right = jnp.concatenate([k, flat(dk_ref)], axis=1)
    d_scores = dot_nt(left, right) * scale
    shift = jnp.sum(probs * d_scores, axis=-1, keepdims=True)
    d_low = (probs * (d_scores - shift)).astype(jnp.bfloat16)
    tangent = (dot(d_low, v) + dot(low, flat(dv_ref))).astype(jnp.bfloat16)
    attended = dot(low, v).astype(jnp.bfloat16)
    mixed_ref[...] = (
        attended.astype(jnp.float32) + coef_ref[0] * tangent.astype(jnp.float32)
    ).astype(jnp.bfloat16)


def attention_specs(seq_count, tokens, arrays, head=0):
    per = ROWS // tokens
    query = lambda n: pl.BlockSpec((per, 1, tokens, HEAD), lambda h, i: (i, n, 0, h + head))
    whole = lambda n: pl.BlockSpec(
        (seq_count, 1, tokens, HEAD), lambda h, i: (0, n, 0, h + head)
    )
    return [query(0), whole(1), whole(2)] * arrays


def attend(qkv, head, scale):
    seq_count, _, tokens, _ = qkv.shape
    length = seq_count * tokens
    return pl.pallas_call(
        functools.partial(forward_kernel, scale),
        grid=(1, length // ROWS),
        in_specs=attention_specs(seq_count, tokens, 1, head),
        out_specs=pl.BlockSpec((HEAD, ROWS), lambda h, i: (h, i)),
        out_shape=jax.ShapeDtypeStruct((HEAD, length), jnp.bfloat16),
        compiler_params=pltpu.CompilerParams(vmem_limit_bytes=8 << 20),
        cost_estimate=pl.CostEstimate(
            flops=4 * length * length * HEAD, bytes_accessed=2 << 20, transcendentals=length * length
        ),
        name="attend",
    )(qkv, qkv, qkv)


def attend_tangent(coef, qkv, d_qkv, scale):
    seq_count, _, tokens, width = qkv.shape
    length = seq_count * tokens
    return pl.pallas_call(
        functools.partial(tangent_kernel, scale),
        grid=(width // HEAD, length // ROWS),
        in_specs=[pl.BlockSpec(memory_space=pltpu.SMEM)] + attention_specs(seq_count, tokens, 2),
        out_specs=pl.BlockSpec((ROWS, HEAD), lambda h, i: (i, h)),
        out_shape=jax.ShapeDtypeStruct((length, width), jnp.bfloat16),
        compiler_params=pltpu.CompilerParams(vmem_limit_bytes=12 << 20),
        cost_estimate=pl.CostEstimate(
            flops=14 * length * length * width, bytes_accessed=8 << 20, transcendentals=length * length * 2
        ),
        name="tangent",
    )(coef, qkv, qkv, qkv, d_qkv, d_qkv, d_qkv)


def gram_kernel(weight_ref, at_ref, *refs):
    blocks, (own, other), out_ref = refs[: 4 * HALVES], refs[4 * HALVES : -2], refs[-1]
    near, depth, cols = out_ref.shape
    zh, core = at_ref[0], at_ref[1]
    part = blocks[0].shape[0] * HALVES // near
    span = near // HALVES
    peak = jnp.zeros((1, 1), jnp.float32)
    for n, step in enumerate(STEPS):
        chip = lax.rem(zh + step, 4)
        for half in range(HALVES):
            left = blocks[n * HALVES + half][...]
            for mixed_ref, side in ((own, core), (other, 1 - core)):
                block = weight_ref[0] * dot(left, mixed_ref[...])
                start = pl.multiple_of((chip * 2 + side) * part, part)
                out_ref[half * span : (half + 1) * span, pl.ds(start, part)] = block.reshape(
                    span, part, cols
                )
                peak = jnp.maximum(peak, jnp.max(jnp.abs(block), keepdims=True))
    out_ref[:, depth - 8 :] = jnp.broadcast_to(peak, (near, 8, cols))


def gram(weight, blocks, mixed, pieces, after):
    rows, cols = blocks[0].shape[0], mixed[0].shape[1]
    depth = 2 * len(blocks) * rows // pieces + 8
    at = jnp.stack([lax.axis_index("zh"), lax.axis_index("core")]).astype(jnp.int32)
    smem = pl.BlockSpec(memory_space=pltpu.SMEM)
    vmem = pl.BlockSpec(memory_space=pltpu.VMEM)
    return pl.pallas_call(
        gram_kernel,
        in_specs=[smem, smem] + [vmem] * (len(blocks) + 2) + [pl.BlockSpec(memory_space=pl.ANY)],
        out_specs=vmem,
        out_shape=jax.ShapeDtypeStruct((pieces, depth, cols), jnp.float32),
        compiler_params=pltpu.CompilerParams(vmem_limit_bytes=12 << 20),
        name="gram",
    )(weight, at, *blocks, *mixed, after)


def finish_kernel(factor, g_ref, w_ref, out_ref):
    total = jnp.zeros(out_ref.shape, jnp.float32)
    for n in range(g_ref.shape[0]):
        high = g_ref[n].astype(jnp.bfloat16)
        rest = (g_ref[n] - high.astype(jnp.float32)).astype(jnp.bfloat16)
        total = total + dot(high, w_ref[n]) + dot(rest, w_ref[n])
    out_ref[...] = total * factor


def finish(g, w, factor):
    return pl.pallas_call(
        functools.partial(finish_kernel, factor),
        out_shape=jax.ShapeDtypeStruct((g.shape[1], w.shape[2]), jnp.float32),
        compiler_params=pltpu.CompilerParams(vmem_limit_bytes=8 << 20),
        name="finish",
    )(g, w)


def shift(x, step):
    n = lax.axis_size("zh")
    return lax.ppermute(x, "zh", [(i, (i + step) % n) for i in range(n)])


def swap(x):
    return lax.ppermute(x, "core", [(0, 1), (1, 0)])


def neighbours(x):
    return shift(x, 1), shift(x, -1)


def settle(x):
    pairs = []
    for y in range(0, lax.axis_size("y"), 2):
        low, high = y * 2 + 1, (y + 1) * 2
        pairs += [(low, high), (high, low)]
    moved = lax.ppermute(x, ("y", "core"), pairs)
    stays = lax.axis_index("y") % 2 == lax.axis_index("core")
    return jnp.where(stays, x, moved)


def exchange(x, axes):
    return lax.all_to_all(x, axes, split_axis=0, concat_axis=0, tiled=True)


def by_heads(arrays, seq_count):
    return jnp.stack(
        [x.reshape(x.shape[0], seq_count, -1).transpose(1, 0, 2) for x in arrays], axis=1
    )


def reduce_near(term):
    count = term.shape[1] - 8
    power = jnp.ceil(jnp.log2(jnp.maximum(term[0, count, 0], 1e-30))) - 15.0
    row = lax.broadcasted_iota(jnp.int32, term.shape, 1)
    held = jnp.where(row < count, term * jnp.exp2(-power), power).astype(jnp.float16)
    parts = exchange(held, NEAR).astype(jnp.float32)
    return jnp.sum(parts[:, :count] * jnp.exp2(parts[:, count : count + 1, :1]), axis=0)


def shards(
    queries, keys, values, d_queries, d_keys, d_values, out_weight, tangent_coef, loss_weight
):
    seq_count = lax.axis_size(SEQ)
    dp_count = lax.axis_size(DP)
    length = queries.shape[0] * seq_count
    scale = 1.0 / HEAD**0.5

    qkv = by_heads((queries, keys, values), seq_count)
    d_qkv = by_heads((d_queries, d_keys, d_values), seq_count)
    weight_part = lax.all_gather(out_weight, "x", axis=0)
    d_qkv, weight_part = lax.optimization_barrier((d_qkv, weight_part))
    weight_part = lax.all_gather(weight_part, "zl", axis=1)
    weight_part = weight_part.reshape(-1, out_weight.shape[1])
    d_qkv, weight_part = lax.optimization_barrier((d_qkv, weight_part))
    weight_all = lax.all_gather(weight_part, "y", axis=0, tiled=True)
    qkv, d_qkv = exchange(qkv, SEQ), exchange(d_qkv, SEQ)
    first, second = attend(qkv, 0, scale), attend(qkv, 1, scale)
    before_first, after_first = neighbours(first)
    before_second, after_second = neighbours(second)
    mixed = attend_tangent(tangent_coef, qkv, d_qkv, scale)
    before_first, before_second, after_first, after_second, mixed = lax.optimization_barrier(
        (before_first, before_second, after_first, after_second, mixed)
    )
    mixed_pair = (mixed, swap(mixed))
    far_first, far_second = shift(before_first, 1), shift(after_second, -1)
    blocks = (
        first, second, before_first, before_second,
        after_first, after_second, far_first, far_second,
    )
    term = gram(loss_weight, blocks, mixed_pair, lax.axis_size(NEAR), weight_all[:16, :HEAD])
    summed = reduce_near(term).reshape(lax.axis_size("y"), -1, mixed.shape[1])
    summed = settle(jnp.sum(exchange(summed, "y"), axis=0))
    rows = lax.all_gather(summed, SEQ, axis=0)
    total_tokens = length * dp_count
    return finish(
        rows, weight_all.reshape(seq_count, mixed.shape[1], -1), LOSS_SCALE / total_tokens**0.5
    )


def solution(mesh):
    split = Mesh(mesh.devices.reshape(8, 4, 2, 4, 2), DP + SEQ)
    tokens = P(DP + SEQ, None)
    placed = (tokens,) * 6 + (P(DP, SEQ), P(DP), P(DP))
    return jax.shard_map(
        shards, mesh=split, in_specs=placed, out_specs=P(DP, SEQ), check_vma=False
    )
```
